256 devices in a mesh: sec: 64 (over x, z_lo, y, core), op: 4 (over z_hi).
Axes of the slice: x: 4, y: 4, z: 8 (z_hi: 4, z_lo: 2; z = z_hi * 2 + z_lo), core: 2. Of those that a mesh axis runs over, the one named last changes fastest.
Arguments:
- psi: bfloat16 [64, 512, 512], P('sec', 'op'), may hold values from -6 to 6
- left_ops: bfloat16 [24, 64, 512, 512], P(None, 'sec', None, 'op'), may hold values from -0.0546875 to 0.0546875
- right_ops: bfloat16 [24, 64, 512, 512], P(None, 'sec', 'op'), may hold values from -0.25 to 0.25
- sources: int32 [64, 24], P('sec'), may hold values from 0 to 63
- counts: int32 [64], P('sec'), may hold values from 6 to 24, as said below
- dims_left: int32 [64], P('sec'), may hold values from 128 to 512, as said below
- dims_right: int32 [64], P('sec'), may hold values from 128 to 512, as said below
Outputs:
- sigma: bfloat16 [64, 512, 512], P('sec', 'op')
The draws below stay inside these ranges and needn't reach their ends.
Inputs may be any that keep to these rules, and one draw needn't show every extreme that they name: `counts`: some sector has all 24 terms active. `dims_left`: some sector has the full padded dimension. `dims_right`: some sector has the full padded dimension.
All inputs are finite; a program needn't handle non-finite values.
Results may differ from the reference program's by a relative error of at most 0.0049.
Values may be sent and summed in bfloat16 or wider, within the bound.
No kernel may reach another device: no remote copies, remote signals or barrier semaphores. Data moves between devices by JAX's collectives and lax.ppermute only.
A program may use at most 128 MiB of HBM per device.

```python
import jax
import jax.numpy as jnp
from jax import lax

BLK = 512
K = 24
S = 64


def forced_draw(key, low, high):
    first_key, second_key = jax.random.split(key)
    drawn = jax.random.randint(first_key, (S,), low, high + 1)
    location = jax.random.randint(second_key, (), 0, S)
    return drawn.at[location].set(high).astype(jnp.int32)


def draw_counts(key, part):
    return forced_draw(jax.random.fold_in(key, 11), max(K // 4, 1), K)


def draw_dims_left(key, part):
    return forced_draw(jax.random.fold_in(key, 23), BLK // 4, BLK)


def draw_dims_right(key, part):
    return forced_draw(jax.random.fold_in(key, 37), BLK // 4, BLK)


def place_ends(values, stream_key, low, top_value):
    longest = values.shape.index(max(values.shape))
    spots = []
    for shift in (0, 1):
        where = [jax.random.randint(jax.random.fold_in(stream_key, axis), (), 0, length) for axis, length in enumerate(values.shape)]
        where[longest] = (where[longest] + shift) % values.shape[longest]
        spots.append(tuple(where))
    return values.at[spots[0]].set(low).at[spots[1]].set(top_value)


def block_levels(own_key, extent, cuts, least, top_value):
    def one(axis_at, parts):
        draws = jax.random.uniform(jax.random.fold_in(jax.random.fold_in(own_key, 6), axis_at), (parts,), jnp.float32, least / len(cuts), top_value / len(cuts))
        return jnp.repeat(jnp.exp(draws), extent[axis_at] // parts).reshape((-1,) + (1,) * (len(extent) - axis_at - 1))

    level = one(*cuts[0])
    for cut in cuts[1:]:
        level = level * one(*cut)
    return level


def normal_values(own_key, dims, scale, most, shards=(), held_as=jnp.bfloat16):
    values = scale * jax.random.normal(own_key, dims, jnp.float32)
    if shards:
        values = values * block_levels(own_key, dims, shards, -0.22, 0.18)
    return jnp.clip(values, -most, most).astype(held_as)


def setup_inputs(seed: int = 0) -> dict:
    keys = jax.random.split(jax.random.key(seed), 8)
    psi = normal_values(keys[0], (S, BLK, BLK), 1.0, 6.0, ((0, 64), (1, 4)))
    left_ops = normal_values(keys[1], (K, S, BLK, BLK), (BLK * K) ** -0.5, 0.0546875, ((1, 64), (3, 4)))
    right_ops = normal_values(keys[2], (K, S, BLK, BLK), BLK ** -0.5, 0.25, ((1, 64), (2, 4)))
    sources = place_ends(jax.random.randint(keys[3], (S, K), 0, S), jax.random.fold_in(keys[3], 1), 0, S - 1).astype(jnp.int32)
    counts = draw_counts(jax.random.fold_in(keys[7], 71), 0)
    dims_left = draw_dims_left(jax.random.fold_in(keys[7], 71), 0)
    dims_right = draw_dims_right(jax.random.fold_in(keys[7], 71), 0)
    return dict(psi=psi, left_ops=left_ops, right_ops=right_ops, sources=sources, counts=counts, dims_left=dims_left, dims_right=dims_right)


def reference(psi, left_ops, right_ops, sources, counts, dims_left, dims_right):
    row_ids = lax.broadcasted_iota(jnp.int32, (S, BLK, BLK), 1)
    col_ids = lax.broadcasted_iota(jnp.int32, (S, BLK, BLK), 2)
    inside_mask = (row_ids < dims_left[:, None, None]) & (col_ids < dims_right[:, None, None])
    panel = jnp.where(inside_mask, psi, jnp.zeros_like(psi))

    def one_sector(sector):
        chosen = jnp.take(panel, sources[sector], axis=0)
        right_blocks = right_ops[:, sector]
        image = jnp.einsum("kab,kcb->kac", chosen.astype(jnp.float32), right_blocks.astype(jnp.float32))
        image = image.astype(jnp.bfloat16)
        active = jnp.arange(K, dtype=jnp.int32) < counts[sector]
        image = jnp.where(active[:, None, None], image, jnp.zeros_like(image))
        summed = jnp.einsum("kab,kbc->ac", left_ops[:, sector].astype(jnp.float32), image.astype(jnp.float32))
        summed = jnp.where(inside_mask[sector], summed, jnp.zeros_like(summed))
        return summed.astype(jnp.bfloat16)

    return lax.map(one_sector, jnp.arange(S, dtype=jnp.int32))
```

```python
import functools

import jax
import jax.numpy as jnp
from jax import lax
from jax.experimental import pallas as pl
from jax.experimental.pallas import tpu as pltpu
from jax.sharding import PartitionSpec as P

NX, NL, NY, NC, NZ = 4, 2, 4, 2, 4
F32, BF16 = jnp.float32, jnp.bfloat16
CHUNKS = (2, 1, 3, 0)
GROUPS = ((2, 0), (1,), (3,))


def sec_at(x, l, y, c):
    return ((x % NX * NL + l % NL) * NY + y % NY) * NC + c


def spots():
    return [(x, l, y, c) for x in range(NX) for l in range(NL) for y in range(NY) for c in range(NC)]


def along(value, which, step):
    perm = []
    for x, l, y, c in spots():
        on_y = (c == 0) == (which == 0)
        far = sec_at(x, l, y + step, c) if on_y else sec_at(x + step, l, y, c)
        perm.append((far, sec_at(x, l, y, c)))
    return lax.ppermute(value, "sec", perm)


def other_core(value):
    return lax.ppermute(value, "sec", [(sec_at(x, l, y, 1 - c), sec_at(x, l, y, c)) for x, l, y, c in spots()])


def from_z(value, flip, step):
    perm = []
    for x, l, y, c in spots():
        for z in range(NZ):
            perm.append((sec_at(x, l + flip, y, c) * NZ + (z + step) % NZ, sec_at(x, l, y, c) * NZ + z))
    return lax.ppermute(value, ("sec", "op"), perm)


def to_op(value, step):
    return lax.ppermute(value, "op", [(z, (z + step) % NZ) for z in range(NZ)])


def image_kernel(term_count, piece_ref, slot_ref, count_ref, right_ref, *rest):
    pieces = rest[:10]
    out_ref, panels, rights, panel_sems, right_sems = rest[10:]

    def issue(k, carry):
        pltpu.make_async_copy(right_ref.at[k], rights.at[k], right_sems.at[k]).start()
        for number, piece in enumerate(pieces):

            @pl.when(piece_ref[k] == number)
            def _():
                pltpu.make_async_copy(piece.at[slot_ref[k]], panels.at[k], panel_sems.at[k]).start()

        return carry

    lax.fori_loop(0, term_count, issue, 0)

    def multiply(group, carry):
        for inner in range(4):
            k = group * 4 + inner
            pltpu.make_async_copy(right_ref.at[k], rights.at[k], right_sems.at[k]).wait()
            pltpu.make_async_copy(pieces[0].at[0], panels.at[k], panel_sems.at[k]).wait()
        for inner in range(4):
            k = group * 4 + inner
            product = lax.dot_general(
                panels[k], rights[k], (((1,), (1,)), ((), ())), preferred_element_type=F32
            )
            out_ref[k] = jnp.where(k < count_ref[0], product, jnp.zeros_like(product)).astype(BF16)
        return carry

    lax.fori_loop(0, term_count // 4, multiply, 0)


def image_of(piece_ids, slots, count, right, pieces):
    terms, cols, depth = right.shape
    rows = pieces[0].shape[1]
    smem = pl.BlockSpec(memory_space=pltpu.SMEM)
    return pl.pallas_call(
        functools.partial(image_kernel, terms),
        out_shape=jax.ShapeDtypeStruct((terms, rows, cols), BF16),
        in_specs=[smem] * 3 + [pl.BlockSpec(memory_space=pl.ANY)] * (1 + len(pieces)),
        out_specs=pl.BlockSpec(memory_space=pltpu.VMEM),
        scratch_shapes=[
            pltpu.VMEM((terms, rows, depth), BF16),
            pltpu.VMEM((terms, cols, depth), BF16),
            pltpu.SemaphoreType.DMA((terms,)),
            pltpu.SemaphoreType.DMA((terms,)),
        ],
        compiler_params=pltpu.CompilerParams(vmem_limit_bytes=32 * 1024 * 1024),
        cost_estimate=pl.CostEstimate(
            flops=2 * terms * rows * cols * depth, bytes_accessed=2 * terms * depth * (rows + cols), transcendentals=0
        ),
    )(piece_ids, slots, count, right, *pieces)


def left_kernel(chunk_count, place_ref, left_ref, *rest):
    images = rest[:chunk_count]
    outs = rest[chunk_count : chunk_count + NZ]
    total = rest[-1]
    step = pl.program_id(0)

    @pl.when(step == 0)
    def _():
        total[...] = jnp.zeros_like(total)

    for pair in range(left_ref.shape[0] // 2):
        left = jnp.concatenate([left_ref[2 * pair], left_ref[2 * pair + 1]], axis=1)
        depth = left.shape[1]
        for number in range(chunk_count):
            image = images[number][2 * pair : 2 * pair + 2].reshape(depth, -1)
            total[number] += jnp.dot(left, image, preferred_element_type=F32)

    @pl.when(step == pl.num_programs(0) - 1)
    def _():
        rows = outs[0].shape[1]
        for e in range(NZ):
            start = pl.multiple_of(lax.rem(place_ref[0] + e, NZ) * rows, rows)
            outs[e][...] = total[:, pl.ds(start, rows), :]


def left_of(place, left, images):
    terms, rows, depth = left.shape
    cols = images[0].shape[2]
    block = 4
    count = len(images)
    part = (count, rows // NZ, cols)
    return pl.pallas_call(
        functools.partial(left_kernel, count),
        grid=(terms // block,),
        out_shape=[jax.ShapeDtypeStruct(part, F32)] * NZ,
        in_specs=[pl.BlockSpec(memory_space=pltpu.SMEM), pl.BlockSpec((block, rows, depth), lambda k: (k, 0, 0))]
        + [pl.BlockSpec((block, depth, cols), lambda k: (k, 0, 0))] * count,
        out_specs=[pl.BlockSpec(part, lambda k: (0, 0, 0))] * NZ,
        scratch_shapes=[pltpu.VMEM((count, rows, cols), F32)],
        compiler_params=pltpu.CompilerParams(vmem_limit_bytes=32 * 1024 * 1024),
        cost_estimate=pl.CostEstimate(
            flops=2 * terms * rows * cols * depth * count, bytes_accessed=2 * terms * depth * (rows + cols * count), transcendentals=0
        ),
    )(place, left, *images)


def final_kernel(place_ref, limit_ref, *rest):
    parts, out_ref = rest[:-1], rest[-1]
    rows = out_ref.shape[0]
    cols = out_ref.shape[1] // NZ
    row_ids = place_ref[0] * rows + lax.broadcasted_iota(jnp.int32, (rows, cols), 0)
    for m in range(NZ):
        value = None
        at = 0
        for group in GROUPS:
            for e in range(NZ):
                for number, chunk in enumerate(group):
                    if (e + chunk) % NZ == m:
                        term = parts[at + e][number]
                        value = term if value is None else value + term
            at += NZ
        start = lax.rem(place_ref[0] + NZ - m, NZ) * cols
        start = pl.multiple_of(start, cols)
        col_ids = start + lax.broadcasted_iota(jnp.int32, (rows, cols), 1)
        inside = (row_ids < limit_ref[0]) & (col_ids < limit_ref[1])
        out_ref[:, pl.ds(start, cols)] = jnp.where(inside, value, jnp.zeros_like(value)).astype(BF16)


def body(psi, left_ops, right_ops, sources, counts, dims_left, dims_right):
    rows, width = psi.shape[1:]
    sec, place = lax.axis_index("sec"), lax.axis_index("op")
    x, l, y, c = sec // (NL * NY * NC), sec // (NY * NC) % NL, sec // NC % NY, sec % NC
    row_ids = place * rows + lax.broadcasted_iota(jnp.int32, (rows, width), 0)
    col_ids = lax.broadcasted_iota(jnp.int32, (rows, width), 1)
    inside = (row_ids < dims_left[0]) & (col_ids < dims_right[0])
    panel = jnp.where(inside, psi[0], jnp.zeros_like(psi[0]))[None]
    place_in = place.astype(jnp.int32)[None]

    s = sources[0]
    dx, dl = (s // (NL * NY * NC) - x) % NX, (s // (NY * NC) - l) % NL
    dy, sc = (s // NC - y) % NY, s % NC
    near = jnp.where(sc == 0, dy, dx)
    far = jnp.where(sc == 0, dx, dy)
    number = jnp.where(far == 2, jnp.where(near < 2, 3, 4), jnp.where(far == 3, 2, far))
    slots = (jnp.where((far == 2) & (near >= 2), near - 2, near) * NL + dl).astype(jnp.int32)
    piece_ids = (number + 5 * ((sc - c) % NC)).astype(jnp.int32)

    pairs = {}
    for j in CHUNKS:
        mine = panel if j == 0 else from_z(panel, 0, j)
        pairs[j] = jnp.concatenate([mine, from_z(panel, 1, j)], axis=0)
    images = {}
    for j in CHUNKS:
        pair = pairs[j]
        block = jnp.concatenate([pair, along(pair, 0, 1), along(pair, 0, 2), along(pair, 0, 3)], axis=0)
        up, down = along(block, 1, 1), along(block, 1, 3)
        half = block.shape[0] // 2
        across_a, across_b = along(up[:half], 1, 1), along(down[half:], 1, 3)
        own = [block, up, down, across_a, across_b]
        pieces = own + [other_core(piece) for piece in own]
        image = image_of(piece_ids, slots, counts, right_ops[:, 0], pieces)
        images[j] = image if j == 0 else to_op(image, j)
    parts = []
    for group in GROUPS:
        outs = left_of(place_in, left_ops[:, 0], [images[j] for j in group])
        parts += [outs[0]] + [to_op(outs[e], e) for e in range(1, NZ)]
    smem = pl.BlockSpec(memory_space=pltpu.SMEM)
    limits = jnp.concatenate([dims_left, dims_right])
    return pl.pallas_call(
        final_kernel,
        out_shape=jax.ShapeDtypeStruct((rows, width), BF16),
        in_specs=[smem] * 2 + [pl.BlockSpec(memory_space=pltpu.VMEM)] * len(parts),
        out_specs=pl.BlockSpec(memory_space=pltpu.VMEM),
    )(place_in, limits, *parts)[None]


def solution(mesh):
    return jax.shard_map(
        body,
        mesh=mesh,
        in_specs=(
            P("sec", "op", None),
            P(None, "sec", None, "op"),
            P(None, "sec", "op", None),
            P("sec", None),
            P("sec"),
            P("sec"),
            P("sec"),
        ),
        out_specs=P("sec", "op", None),
        check_vma=False,
    )
```

```python
import functools

import jax
import jax.numpy as jnp
from jax import lax
from jax.experimental import pallas as pl
from jax.experimental.pallas import tpu as pltpu
from jax.sharding import Mesh
from jax.sharding import PartitionSpec as P

NX, NL, NY, NC, NZ = 4, 2, 4, 2, 4
F32, BF16 = jnp.float32, jnp.bfloat16
SEC = ("x", "l", "y", "c")
SHARE = 4
WIRE = BF16
VMEM_LIMIT = 40 * 1024 * 1024
ANY = pl.BlockSpec(memory_space=pl.ANY)
SMEM = pl.BlockSpec(memory_space=pltpu.SMEM)
VMEM = pl.BlockSpec(memory_space=pltpu.VMEM)
PARAMS = pltpu.CompilerParams(vmem_limit_bytes=VMEM_LIMIT)


def along(value, which, step):
    perm = []
    for x in range(NX):
        for y in range(NY):
            for c in range(NC):
                on_y = (c == 0) == (which == 0)
                far = (x, (y + step) % NY) if on_y else ((x + step) % NX, y)
                perm.append(((far[0] * NY + far[1]) * NC + c, (x * NY + y) * NC + c))
    return lax.ppermute(value, ("x", "y", "c"), perm)


def swap(value, axis):
    return lax.ppermute(value, axis, [(0, 1), (1, 0)])


def from_op(value, step):
    return lax.ppermute(value, "z", [((z + step) % NZ, z) for z in range(NZ)])


def after(value, *others):
    return lax.optimization_barrier((value,) + others)[0]


def fetch(k, at, facts, pieces, panels, sems):
    own_pieces, other_pieces = pieces[:2], pieces[2:]
    for number, piece in enumerate(own_pieces):

        @pl.when(facts[0, k] == number)
        def _():
            pltpu.make_async_copy(piece.at[pl.ds(facts[1, k], 1)], panels.at[at, pl.ds(0, 1)], sems.at[at, 0]).start()

    for number, piece in enumerate(other_pieces):

        @pl.when(facts[2, k] == number)
        def _():
            pltpu.make_async_copy(piece.at[pl.ds(facts[3, k], NZ - 1)], panels.at[at, pl.ds(1, NZ - 1)], sems.at[at, 1]).start()


def fetched(at, pieces, panels, sems):
    pltpu.make_async_copy(pieces[0].at[pl.ds(0, 1)], panels.at[at, pl.ds(0, 1)], sems.at[at, 0]).wait()
    pltpu.make_async_copy(pieces[2].at[pl.ds(0, NZ - 1)], panels.at[at, pl.ds(1, NZ - 1)], sems.at[at, 1]).wait()


def product(panel, right, active):
    panel = panel.reshape(panel.shape[0] * panel.shape[1], panel.shape[2])
    value = lax.dot_general(panel, right, (((1,), (1,)), ((), ())), preferred_element_type=F32)
    return jnp.where(active, value, jnp.zeros_like(value)).astype(BF16)


def moving_kernel(first, place_ref, facts, count_ref, right_ref, *rest):
    pieces = rest[:18]
    out_ref, panels, rights, panel_sems, right_sem = rest[18:]
    terms = out_ref.shape[1]
    rights_copy = pltpu.make_async_copy(right_ref.at[pl.ds(first, terms)], rights, right_sem)
    rights_copy.start()

    def start(t, carry):
        fetch(first + t, t, facts, pieces, panels, panel_sems)
        return carry

    lax.fori_loop(0, terms, start, 0)
    rights_copy.wait()

    def step(pair, carry):
        for inner in range(2):
            fetched(pair * 2 + inner, pieces, panels, panel_sems)
        for inner in range(2):
            t = pair * 2 + inner
            value = product(panels[t], rights[t], first + t < count_ref[0])
            rows = value.shape[0] // NZ
            for j in range(NZ):
                out_ref[lax.rem(place_ref[0] + j, NZ), t] = value[j * rows : (j + 1) * rows]
        return carry

    lax.fori_loop(0, terms // 2, step, 0)


def moving_products(first, place, facts, count, right, pieces):
    terms, cols, depth = right.shape
    terms -= first
    return pl.pallas_call(
        functools.partial(moving_kernel, first),
        out_shape=jax.ShapeDtypeStruct((NZ, terms, cols, cols), BF16),
        in_specs=[SMEM] * 3 + [ANY] * 19,
        out_specs=VMEM,
        scratch_shapes=[
            pltpu.VMEM((terms, NZ, cols, depth), BF16),
            pltpu.VMEM((terms, cols, depth), BF16),
            pltpu.SemaphoreType.DMA((terms, 2)),
            pltpu.SemaphoreType.DMA,
        ],
        compiler_params=PARAMS,
        cost_estimate=pl.CostEstimate(flops=2 * terms * cols * depth**2, bytes_accessed=2 * terms * depth**2, transcendentals=0),
    )(place, facts, count, right, *pieces)


def whole_kernel(place_ref, facts, count_ref, *rest):
    rights_in, lefts_in, pieces = rest[0], rest[1], rest[2:20]
    out_ref, panels, rights, lefts, panel_sems, sems = rest[20:]
    share, _, rows, _ = panels.shape
    place = place_ref[0]
    copies = []
    for j in range(NZ):
        home = lax.rem(place + j, NZ)
        copies.append(pltpu.make_async_copy(rights_in.at[j], rights.at[:, pl.ds(j * rows, rows), :], sems.at[0, j]))
        copies.append(pltpu.make_async_copy(lefts_in.at[home], lefts.at[:, :, pl.ds(j * rows, rows)], sems.at[1, j]))
    for copy in copies:
        copy.start()
    for t in range(share):
        fetch(place * share + t, t, facts, pieces, panels, panel_sems)
    for copy in copies:
        copy.wait()
    for t in range(share):
        fetched(t, pieces, panels, panel_sems)
        image = product(panels[t], rights[t], place * share + t < count_ref[0])
        value = jnp.dot(lefts[t], image, preferred_element_type=F32)
        if t == 0:
            out_ref[...] = value
        else:
            out_ref[...] += value


def whole_terms(place, facts, count, rights, lefts, pieces):
    _, share, rows, depth = rights.shape
    return pl.pallas_call(
        whole_kernel,
        out_shape=jax.ShapeDtypeStruct((depth, depth), F32),
        in_specs=[SMEM] * 3 + [ANY] * 20,
        out_specs=VMEM,
        scratch_shapes=[
            pltpu.VMEM((share, NZ, rows, depth), BF16),
            pltpu.VMEM((share, depth, depth), BF16),
            pltpu.VMEM((share, depth, depth), BF16),
            pltpu.SemaphoreType.DMA((share, 2)),
            pltpu.SemaphoreType.DMA((2, NZ)),
        ],
        compiler_params=PARAMS,
        cost_estimate=pl.CostEstimate(flops=4 * share * depth**3, bytes_accessed=6 * share * depth**2, transcendentals=0),
    )(place, facts, count, rights, lefts, *pieces)


def gather_kernel(first, left_ref, sum_ref, images, out_ref, lefts, moved, sems):
    _, terms, rows, cols = images.shape
    copies = [
        pltpu.make_async_copy(left_ref.at[first + t], lefts.at[:, pl.ds(t * rows, rows)], sems.at[t]) for t in range(terms)
    ]
    for copy in copies:
        copy.start()
    for j in range(NZ):
        moved[:, j * cols : (j + 1) * cols] = images[j].reshape(terms * rows, cols)
    for copy in copies:
        copy.wait()
    for e in range(NZ):
        span = slice(e * rows, (e + 1) * rows)
        value = sum_ref[span, :] + jnp.dot(lefts[span, :], moved[...], preferred_element_type=F32)
        out_ref[e] = value.astype(out_ref.dtype)


def gather_terms(first, left, total, images):
    _, terms, rows, cols = images.shape
    width = total.shape[1]
    return pl.pallas_call(
        functools.partial(gather_kernel, first),
        out_shape=jax.ShapeDtypeStruct((NZ, rows, width), WIRE),
        in_specs=[ANY, VMEM, VMEM],
        out_specs=VMEM,
        scratch_shapes=[
            pltpu.VMEM((total.shape[0], terms * rows), BF16),
            pltpu.VMEM((terms * rows, width), BF16),
            pltpu.SemaphoreType.DMA((terms,)),
        ],
        compiler_params=PARAMS,
        cost_estimate=pl.CostEstimate(flops=2 * terms * rows * width**2, bytes_accessed=4 * width**2, transcendentals=0),
    )(left, total, images)


def final_kernel(place_ref, limit_ref, parts, out_ref):
    shape = out_ref.shape
    value = parts[0].astype(F32)
    for source in range(1, NZ):
        value = value + parts[source].astype(F32)
    row_ids = place_ref[0] * shape[0] + lax.broadcasted_iota(jnp.int32, shape, 0)
    col_ids = lax.broadcasted_iota(jnp.int32, shape, 1)
    inside = (row_ids < limit_ref[0]) & (col_ids < limit_ref[1])
    out_ref[...] = jnp.where(inside, value, jnp.zeros_like(value)).astype(BF16)


def body(psi, left_ops, right_ops, sources, counts, dims_left, dims_right):
    rows, width = psi.shape[1:]
    right, left = right_ops[:, 0], left_ops[:, 0]
    x, l, y, c, place = (lax.axis_index(name) for name in ("x", "l", "y", "c", "z"))
    row_ids = place * rows + lax.broadcasted_iota(jnp.int32, (rows, width), 0)
    col_ids = lax.broadcasted_iota(jnp.int32, (rows, width), 1)
    inside = (row_ids < dims_left[0]) & (col_ids < dims_right[0])
    panel = jnp.where(inside, psi[0], jnp.zeros_like(psi[0]))[None]
    place_in = place.astype(jnp.int32)[None]

    pair = jnp.concatenate([panel, swap(panel, "l")], axis=0)
    others = [from_op(pair, j) for j in range(1, NZ)]
    own = jnp.concatenate([pair] + [along(pair, 0, step) for step in (1, 2, 3)], axis=0)
    own_up, own_down = along(own, 1, 1), along(own, 1, 3)
    half = own.shape[0] // 2
    own_across = [along(own_up[:half], 1, 1), along(own_down[half:], 1, 3)]
    own = jnp.concatenate([own, own_up, own_down] + own_across, axis=0)
    own_there = swap(own, "c")
    stack = jnp.stack(others, axis=1).reshape(NL * (NZ - 1), rows, width)
    near = [stack] + [along(stack, 0, step) for step in (1, 2, 3)]
    low = jnp.concatenate(near[:2], axis=0)
    high = after(jnp.concatenate(near[2:], axis=0), *own_across)
    up_low, down_high = along(low, 1, 1), along(high, 1, 3)

    first = SHARE * NZ
    right_late = after(right[:first], *others)
    rights = lax.all_to_all(right_late.reshape(NZ, SHARE, rows, width), "z", 0, 0, tiled=True)
    left_late = after(left[:first], rights)
    lefts = lax.all_to_all(left_late.reshape(NZ, SHARE, width, rows), "z", 0, 0, tiled=True)

    up_high, down_low = along(high, 1, 1), along(low, 1, 3)
    a, b, *_ = lax.optimization_barrier((up_low, down_high, rights, own_there))
    across_low, across_high = along(a, 1, 1), along(b, 1, 3)
    early = [swap(piece, "c") for piece in (low, high, up_low, up_high, down_low, down_high)]
    c_low, c_high, *_ = lax.optimization_barrier((across_low, across_high, lefts, *early))
    others_here = [low, high, up_low, up_high, across_low, across_high, down_low, down_high]
    others_there = early[:4] + [swap(c_low, "c"), swap(c_high, "c")] + early[4:]
    pieces = [own, own_there] + others_here + others_there

    s = sources[0]
    sx, sl, sy, sc = s // (NL * NY * NC), s // (NY * NC) % NL, s // NC % NY, s % NC
    dx, dl, dy, dc = (sx - x) % NX, (sl - l) % NL, (sy - y) % NY, (sc - c) % NC
    near, far = jnp.where(sc == 0, dy, dx), jnp.where(sc == 0, dx, dy)
    own_slot = (jnp.where(far == 2, 3, jnp.where(far == 3, 2, far)) * 4 + near) * NL + dl
    piece = far * 2 + near // 2 + 8 * dc
    slot = (near % 2 * NL + dl) * (NZ - 1)
    facts = jnp.stack([dc, own_slot, piece, slot]).astype(jnp.int32)

    images = moving_products(first, place_in, facts, counts, right, pieces)
    total = whole_terms(place_in, after(facts, images), counts, rights, lefts, pieces)
    images = lax.all_to_all(images, "z", 0, 0, tiled=True)
    parts = lax.all_to_all(gather_terms(first, left, total, images), "z", 0, 0, tiled=True)
    limits = jnp.concatenate([dims_left, dims_right])
    return pl.pallas_call(
        final_kernel,
        out_shape=jax.ShapeDtypeStruct((rows, width), BF16),
        in_specs=[SMEM] * 2 + [VMEM],
        out_specs=VMEM,
    )(place_in, limits, parts)[None]


def solution(mesh):
    parts = Mesh(mesh.devices.reshape(NX, NL, NY, NC, NZ), SEC + ("z",))
    return jax.shard_map(
        body,
        mesh=parts,
        in_specs=(
            P(SEC, "z", None),
            P(None, SEC, None, "z"),
            P(None, SEC, "z", None),
            P(SEC, None),
            P(SEC),
            P(SEC),
            P(SEC),
        ),
        out_specs=P(SEC, "z", None),
        check_vma=False,
    )
```

```python
import functools

import jax
import jax.numpy as jnp
from jax import lax
from jax.experimental import pallas as pl
from jax.experimental.pallas import tpu as pltpu
from jax.sharding import Mesh
from jax.sharding import PartitionSpec as P

NX, NL, NY, NC, NZ = 4, 2, 4, 2, 4
F32, BF16 = jnp.float32, jnp.bfloat16
SEC = ("x", "l", "y", "c")
SHARE = 5
WIRE = BF16
VMEM_LIMIT = 40 * 1024 * 1024
ANY = pl.BlockSpec(memory_space=pl.ANY)
SMEM = pl.BlockSpec(memory_space=pltpu.SMEM)
VMEM = pl.BlockSpec(memory_space=pltpu.VMEM)
PARAMS = pltpu.CompilerParams(vmem_limit_bytes=VMEM_LIMIT)


def along(value, which, step):
    perm = []
    for x in range(NX):
        for y in range(NY):
            for c in range(NC):
                on_y = (c == 0) == (which == 0)
                far = (x, (y + step) % NY) if on_y else ((x + step) % NX, y)
                perm.append(((far[0] * NY + far[1]) * NC + c, (x * NY + y) * NC + c))
    return lax.ppermute(value, ("x", "y", "c"), perm)


def swap(value, axis):
    return lax.ppermute(value, axis, [(0, 1), (1, 0)])


def from_op(value, step):
    return lax.ppermute(value, "z", [((z + step) % NZ, z) for z in range(NZ)])


def after(value, *others):
    return lax.optimization_barrier((value,) + others)[0]


def fetch(k, at, facts, pieces, panels, sems):
    own_pieces, other_pieces = pieces[:2], pieces[2:]
    for number, piece in enumerate(own_pieces):

        @pl.when(facts[0, k] == number)
        def _():
            pltpu.make_async_copy(piece.at[pl.ds(facts[1, k], 1)], panels.at[at, pl.ds(0, 1)], sems.at[at, 0]).start()

    for number, piece in enumerate(other_pieces):

        @pl.when(facts[2, k] == number)
        def _():
            pltpu.make_async_copy(piece.at[pl.ds(facts[3, k], NZ - 1)], panels.at[at, pl.ds(1, NZ - 1)], sems.at[at, 1]).start()


def fetched(at, pieces, panels, sems):
    pltpu.make_async_copy(pieces[0].at[pl.ds(0, 1)], panels.at[at, pl.ds(0, 1)], sems.at[at, 0]).wait()
    pltpu.make_async_copy(pieces[2].at[pl.ds(0, NZ - 1)], panels.at[at, pl.ds(1, NZ - 1)], sems.at[at, 1]).wait()


def product(panel, right, active):
    panel = panel.reshape(panel.shape[0] * panel.shape[1], panel.shape[2])
    value = lax.dot_general(panel, right, (((1,), (1,)), ((), ())), preferred_element_type=F32)
    return jnp.where(active, value, jnp.zeros_like(value)).astype(BF16)


def moving_kernel(first, place_ref, facts, count_ref, right_ref, *rest):
    pieces = rest[:18]
    out_ref, panels, rights, panel_sems, right_sem = rest[18:]
    terms = out_ref.shape[1]
    rights_copy = pltpu.make_async_copy(right_ref.at[pl.ds(first, terms)], rights, right_sem)
    rights_copy.start()

    def start(t, carry):
        fetch(first + t, t, facts, pieces, panels, panel_sems)
        return carry

    lax.fori_loop(0, terms, start, 0)
    rights_copy.wait()

    def step(pair, carry):
        for inner in range(2):
            fetched(pair * 2 + inner, pieces, panels, panel_sems)
        for inner in range(2):
            t = pair * 2 + inner
            value = product(panels[t], rights[t], first + t < count_ref[0])
            rows = value.shape[0] // NZ
            for j in range(NZ):
                out_ref[lax.rem(place_ref[0] + j, NZ), t] = value[j * rows : (j + 1) * rows]
        return carry

    lax.fori_loop(0, terms // 2, step, 0)


def moving_products(first, place, facts, count, right, pieces):
    terms, cols, depth = right.shape
    terms -= first
    return pl.pallas_call(
        functools.partial(moving_kernel, first),
        out_shape=jax.ShapeDtypeStruct((NZ, terms, cols, cols), BF16),
        in_specs=[SMEM] * 3 + [ANY] * 19,
        out_specs=VMEM,
        scratch_shapes=[
            pltpu.VMEM((terms, NZ, cols, depth), BF16),
            pltpu.VMEM((terms, cols, depth), BF16),
            pltpu.SemaphoreType.DMA((terms, 2)),
            pltpu.SemaphoreType.DMA,
        ],
        compiler_params=PARAMS,
        cost_estimate=pl.CostEstimate(flops=2 * terms * cols * depth**2, bytes_accessed=2 * terms * depth**2, transcendentals=0),
    )(place, facts, count, right, *pieces)


def whole_kernel(place_ref, facts, count_ref, *rest):
    operators, pieces = rest[0], rest[1:19]
    out_ref, panels, rights, lefts, panel_sems, sems = rest[19:]
    share, _, rows, _ = panels.shape
    place = place_ref[0]
    copies = []
    for j in range(NZ):
        home = lax.rem(place + j, NZ)
        there = rights.at[:, pl.ds(j * rows, rows), :]
        copies.append(pltpu.make_async_copy(operators.at[j, pl.ds(0, share)], there, sems.at[NZ, j]))
        for m in range(NZ):
            here = operators.at[home, pl.ds(share, share), :, pl.ds(m * rows, rows)]
            there = lefts.at[:, pl.ds(m * rows, rows), pl.ds(j * rows, rows)]
            copies.append(pltpu.make_async_copy(here, there, sems.at[m, j]))
    for copy in copies:
        copy.start()
    for t in range(share):
        fetch(place * share + t, t, facts, pieces, panels, panel_sems)
    for copy in copies:
        copy.wait()
    for t in range(share):
        fetched(t, pieces, panels, panel_sems)
        image = product(panels[t], rights[t], place * share + t < count_ref[0])
        value = jnp.dot(lefts[t], image, preferred_element_type=F32)
        if t == 0:
            out_ref[...] = value
        else:
            out_ref[...] += value


def whole_terms(place, facts, count, operators, pieces):
    _, share, rows, depth = operators.shape
    share //= 2
    return pl.pallas_call(
        whole_kernel,
        out_shape=jax.ShapeDtypeStruct((depth, depth), F32),
        in_specs=[SMEM] * 3 + [ANY] * 19,
        out_specs=VMEM,
        scratch_shapes=[
            pltpu.VMEM((share, NZ, rows, depth), BF16),
            pltpu.VMEM((share, depth, depth), BF16),
            pltpu.VMEM((share, depth, depth), BF16),
            pltpu.SemaphoreType.DMA((share, 2)),
            pltpu.SemaphoreType.DMA((NZ + 1, NZ)),
        ],
        compiler_params=PARAMS,
        cost_estimate=pl.CostEstimate(flops=4 * share * depth**3, bytes_accessed=6 * share * depth**2, transcendentals=0),
    )(place, facts, count, operators, *pieces)


def gather_kernel(first, left_ref, sum_ref, images, out_ref, lefts, moved, sems):
    _, terms, rows, cols = images.shape
    copies = [
        pltpu.make_async_copy(left_ref.at[first + t], lefts.at[:, pl.ds(t * rows, rows)], sems.at[t]) for t in range(terms)
    ]
    for copy in copies:
        copy.start()
    for j in range(NZ):
        moved[:, j * cols : (j + 1) * cols] = images[j].reshape(terms * rows, cols)
    for copy in copies:
        copy.wait()
    for e in range(NZ):
        span = slice(e * rows, (e + 1) * rows)
        value = sum_ref[span, :] + jnp.dot(lefts[span, :], moved[...], preferred_element_type=F32)
        out_ref[e] = value.astype(out_ref.dtype)


def gather_terms(first, left, total, images):
    _, terms, rows, cols = images.shape
    width = total.shape[1]
    return pl.pallas_call(
        functools.partial(gather_kernel, first),
        out_shape=jax.ShapeDtypeStruct((NZ, rows, width), WIRE),
        in_specs=[ANY, VMEM, VMEM],
        out_specs=VMEM,
        scratch_shapes=[
            pltpu.VMEM((total.shape[0], terms * rows), BF16),
            pltpu.VMEM((terms * rows, width), BF16),
            pltpu.SemaphoreType.DMA((terms,)),
        ],
        compiler_params=PARAMS,
        cost_estimate=pl.CostEstimate(flops=2 * terms * rows * width**2, bytes_accessed=4 * width**2, transcendentals=0),
    )(left, total, images)


def final_kernel(place_ref, limit_ref, parts, out_ref):
    shape = out_ref.shape
    value = parts[0].astype(F32)
    for source in range(1, NZ):
        value = value + parts[source].astype(F32)
    row_ids = place_ref[0] * shape[0] + lax.broadcasted_iota(jnp.int32, shape, 0)
    col_ids = lax.broadcasted_iota(jnp.int32, shape, 1)
    inside = (row_ids < limit_ref[0]) & (col_ids < limit_ref[1])
    out_ref[...] = jnp.where(inside, value, jnp.zeros_like(value)).astype(BF16)


def body(psi, left_ops, right_ops, sources, counts, dims_left, dims_right):
    rows, width = psi.shape[1:]
    right, left = right_ops[:, 0], left_ops[:, 0]
    x, l, y, c, place = (lax.axis_index(name) for name in ("x", "l", "y", "c", "z"))
    row_ids = place * rows + lax.broadcasted_iota(jnp.int32, (rows, width), 0)
    col_ids = lax.broadcasted_iota(jnp.int32, (rows, width), 1)
    inside = (row_ids < dims_left[0]) & (col_ids < dims_right[0])
    panel = jnp.where(inside, psi[0], jnp.zeros_like(psi[0]))[None]
    place_in = place.astype(jnp.int32)[None]

    pair = jnp.concatenate([panel, swap(panel, "l")], axis=0)
    others = [from_op(pair, j) for j in range(1, NZ)]
    first = SHARE * NZ
    wide = jnp.concatenate([left[:first, m * rows : (m + 1) * rows] for m in range(NZ)], axis=2)
    both = jnp.concatenate([v.reshape(NZ, SHARE, rows, width) for v in (right[:first], wide)], axis=1)
    whole = lax.all_to_all(after(both, *others), "z", 0, 0, tiled=True)
    own = jnp.concatenate([pair] + [along(pair, 0, step) for step in (1, 2, 3)], axis=0)
    own_up, own_down = along(own, 1, 1), along(own, 1, 3)
    half = own.shape[0] // 2
    own_across = [along(own_up[:half], 1, 1), along(own_down[half:], 1, 3)]
    own = jnp.concatenate([own, own_up, own_down] + own_across, axis=0)
    own_there = swap(after(own, whole), "c")
    stack = jnp.stack(others, axis=1).reshape(NL * (NZ - 1), rows, width)
    near = [stack] + [along(stack, 0, step) for step in (1, 2, 3)]
    low = jnp.concatenate(near[:2], axis=0)
    high = jnp.concatenate(near[2:], axis=0)
    up_low, down_high = along(low, 1, 1), along(high, 1, 3)

    up_high, down_low = along(high, 1, 1), along(low, 1, 3)
    a, b, *_ = (up_low, down_high, None)
    across_low, across_high = along(a, 1, 1), along(b, 1, 3)
    early = [swap(piece, "c") for piece in (low, high, up_low, up_high, down_low, down_high)]
    c_low, c_high, *_ = lax.optimization_barrier((across_low, across_high, *early))
    others_here = [low, high, up_low, up_high, across_low, across_high, down_low, down_high]
    others_there = early[:4] + [swap(c_low, "c"), swap(c_high, "c")] + early[4:]
    pieces = [own, own_there] + others_here + others_there

    s = sources[0]
    sx, sl, sy, sc = s // (NL * NY * NC), s // (NY * NC) % NL, s // NC % NY, s % NC
    dx, dl, dy, dc = (sx - x) % NX, (sl - l) % NL, (sy - y) % NY, (sc - c) % NC
    near, far = jnp.where(sc == 0, dy, dx), jnp.where(sc == 0, dx, dy)
    own_slot = (jnp.where(far == 2, 3, jnp.where(far == 3, 2, far)) * 4 + near) * NL + dl
    piece = far * 2 + near // 2 + 8 * dc
    slot = (near % 2 * NL + dl) * (NZ - 1)
    facts = jnp.stack([dc, own_slot, piece, slot]).astype(jnp.int32)

    images = moving_products(first, place_in, facts, counts, right, pieces)
    total = whole_terms(place_in, after(facts, images), counts, whole, pieces)
    images = lax.all_to_all(images, "z", 0, 0, tiled=True)
    parts = lax.all_to_all(gather_terms(first, left, total, images), "z", 0, 0, tiled=True)
    limits = jnp.concatenate([dims_left, dims_right])
    return pl.pallas_call(
        final_kernel,
        out_shape=jax.ShapeDtypeStruct((rows, width), BF16),
        in_specs=[SMEM] * 2 + [VMEM],
        out_specs=VMEM,
    )(place_in, limits, parts)[None]


def solution(mesh):
    parts = Mesh(mesh.devices.reshape(NX, NL, NY, NC, NZ), SEC + ("z",))
    return jax.shard_map(
        body,
        mesh=parts,
        in_specs=(
            P(SEC, "z", None),
            P(None, SEC, None, "z"),
            P(None, SEC, "z", None),
            P(SEC, None),
            P(SEC),
            P(SEC),
            P(SEC),
        ),
        out_specs=P(SEC, "z", None),
        check_vma=False,
    )
```
